32 devices in a mesh: rows: 4 (over z), cols: 2 (over core), heads: 4 (over y, x).
Axes of the slice: x: 2, y: 2, z: 4, core: 2. Of those that a mesh axis runs over, the one named last changes fastest.
Arguments:
- queries: bfloat16 [256, 32, 1280], P(('rows', 'heads'), 'cols'), may hold values from -5 to 5
- key_rows: bfloat16 [256, 32, 1280], P(('rows', 'heads'), 'cols'), may hold values from -5 to 5
- value_rows: bfloat16 [256, 32, 1280], P(('rows', 'heads'), 'cols'), may hold values from -5 to 5
- out_grad: bfloat16 [256, 32, 1280], P(('rows', 'heads'), 'cols'), may hold values from -5 to 5
- pattern: int32 [32, 4], replicated, may hold values from 0 to 511
- tissue: int32 [32, 4], replicated, may hold values 0 or 1
Outputs:
- query_grad: bfloat16 [256, 32, 1280], P(('rows', 'heads'), 'cols')
- key_grad: bfloat16 [256, 32, 1280], P(('rows', 'heads'), 'cols')
- value_grad: bfloat16 [256, 32, 1280], P(('rows', 'heads'), 'cols')
The draws below stay inside these ranges and needn't reach their ends.
All inputs are finite; a program needn't handle non-finite values.
Results may differ from the reference program's by a relative error of at most 0.0067.
Values may be sent and summed in bfloat16 or wider, within the bound.
A program may use at most 128 MiB of HBM per device.

```python
import math
import jax
import jax.numpy as jnp
from jax import lax

D = 1280
HEADS = 16
HDIM = 80
TILE_SIDE = 8
HT = 256
WT = 32
GRID_TR = 32
GRID_TC = 4


def drawn_base(key, offset):
    return jnp.clip(jax.random.normal(jax.random.fold_in(key, offset), (HT, WT, D), jnp.float32), -5.0, 5.0)


def draw_queries(key, part):
    drawn = drawn_base(key, 1)
    return drawn.astype(jnp.bfloat16)


def draw_key_rows(key, part):
    drawn = drawn_base(key, 5)
    return drawn.astype(jnp.bfloat16)


def place_ends(entries, rng, low, high):
    shape = entries.shape
    index_at = [jax.random.randint(jax.random.fold_in(rng, axis), (), 0, shape[axis]) for axis in range(len(shape))]
    entries = entries.at[tuple(index_at)].set(low)
    longest = shape.index(max(shape))
    index_at[longest] = (index_at[longest] + 1) % shape[longest]
    return entries.at[tuple(index_at)].set(high)


def block_levels(rng, shape, pieces, low, top_value):
    gain = 1.0
    for dim, parts in pieces:
        heights = jax.random.uniform(jax.random.fold_in(jax.random.fold_in(rng, 6), dim), (parts,), jnp.float32, low / len(pieces), top_value / len(pieces))
        gain = gain * jnp.repeat(jnp.exp(heights), shape[dim] // parts).reshape((-1,) + (1,) * (len(shape) - 1 - dim))
    return gain


def gaussian(stream_key, dims, scale, reach, pieces=(), held_as=jnp.bfloat16):
    level = block_levels(stream_key, dims, pieces, -0.22, 0.18) if pieces else 1.0
    entries = jax.random.normal(stream_key, dims, jnp.float32) * scale * level
    return jnp.minimum(jnp.maximum(entries, -reach), reach).astype(held_as)


def setup_inputs(seed: int = 0) -> dict:
    streams_of = jax.random.split(jax.random.key(seed), 7)
    queries = draw_queries(jax.random.fold_in(streams_of[6], 71), 0)
    key_rows = draw_key_rows(jax.random.fold_in(streams_of[6], 71), 0)
    value_rows = gaussian(streams_of[2], (HT, WT, D), 1.0, 5.0, ((0, 16), (1, 2)))
    out_grad = gaussian(streams_of[3], (HT, WT, D), 1.0, 5.0, ((0, 16), (1, 2)))
    pattern = place_ends(jax.random.randint(streams_of[4], (GRID_TR, GRID_TC), 0, 512), jax.random.fold_in(streams_of[4], 1), 0, 511).astype(jnp.int32)
    tissue = place_ends((jax.random.randint(streams_of[5], (GRID_TR, GRID_TC), 0, 4) < 3).astype(jnp.int32), jax.random.fold_in(streams_of[5], 1), 0, 1)
    return {"queries": queries, "key_rows": key_rows, "value_rows": value_rows, "out_grad": out_grad, "pattern": pattern, "tissue": tissue}


def cell_at(indices):
    return tuple((jnp.asarray(item).astype(jnp.int32) for item in indices))

def product(form, left, right):
    return jnp.einsum(form, left.astype(jnp.float32), right.astype(jnp.float32))

def neighbour_mask(pattern, tissue_pad, tile_row, first_col, tile_cols):
    pattern_row = lax.dynamic_slice(pattern, cell_at((tile_row, first_col)), (1, tile_cols))[0]
    tissue_near = lax.dynamic_slice(tissue_pad, cell_at((tile_row, first_col)), (3, tile_cols + 2))
    slots = []
    for a in range(3):
        for b in range(3):
            if a == 1 and b == 1:
                slots.append(pattern_row >= 0)
            else:
                bit_set = jnp.right_shift(pattern_row, 3 * a + b) & 1
                slots.append((bit_set == 1) & (tissue_near[a, b:b + tile_cols] == 1))
    return jnp.stack(slots, 1)

def tile_backward(queries, padded, out_grad, pattern, tissue, first_row, first_col, width):
    tile_side = TILE_SIDE
    row_count, col_count, features = queries.shape
    tile_rows = row_count // tile_side
    tile_cols = col_count // tile_side
    group_heads = width // HDIM
    group_count = features // width
    score_scale = 1.0 / math.sqrt(HDIM)
    tissue_pad = jnp.pad(tissue, 1)

    def tile_step(carried, index):
        query_grads, totals = carried
        tile_row = index // group_count
        group_at = index % group_count * width
        row_at = tile_row * tile_side
        query_tile = lax.dynamic_slice(queries, cell_at((row_at, 0, group_at)), (tile_side, col_count, width))
        query_tile = query_tile.reshape(tile_side, tile_cols, tile_side, group_heads, HDIM)
        grad_tile = lax.dynamic_slice(out_grad, cell_at((row_at, 0, group_at)), (tile_side, col_count, width))
        grad_tile = grad_tile.reshape(tile_side, tile_cols, tile_side, group_heads, HDIM)
        key_band = lax.dynamic_slice(padded, cell_at((row_at, 0, 0, group_at)), (3 * tile_side, col_count + 2 * tile_side, 2, width))
        slot_rows = jnp.stack([key_band[a * tile_side:(a + 1) * tile_side, b * tile_side:b * tile_side + col_count] for a in range(3) for b in range(3)])
        slot_rows = slot_rows.reshape(9, tile_side, tile_cols, tile_side, 2, group_heads, HDIM)
        near_keys = slot_rows[:, :, :, :, 0]
        near_values = slot_rows[:, :, :, :, 1]
        allowed = neighbour_mask(pattern, tissue_pad, first_row + tile_row, first_col, tile_cols)
        scores = product('ujwhd,nyjxhd->jhuwnyx', query_tile, near_keys) * score_scale
        scores = jnp.where(allowed[:, None, None, None, :, None, None], scores, -1e+30)
        row_max = lax.optimization_barrier(jnp.max(scores, axis=(4, 5, 6), keepdims=True))
        exp_scores = jnp.exp(scores - row_max)
        weights = exp_scores / lax.optimization_barrier(jnp.sum(exp_scores, axis=(4, 5, 6), keepdims=True))
        weight_grad = product('ujwhd,nyjxhd->jhuwnyx', grad_tile, near_values)
        row_dot = lax.optimization_barrier(jnp.sum(weights * weight_grad, axis=(4, 5, 6), keepdims=True))
        score_grad = (weights * (weight_grad - row_dot)).astype(jnp.bfloat16)
        weights_low = weights.astype(jnp.bfloat16)
        query_part = product('jhuwnyx,nyjxhd->ujwhd', score_grad, near_keys) * score_scale
        key_part = product('jhuwnyx,ujwhd->nyjxhd', score_grad, query_tile) * score_scale
        value_part = product('jhuwnyx,ujwhd->nyjxhd', weights_low, grad_tile)
        kv_parts = jnp.stack([key_part, value_part], 4).reshape(3, 3, tile_side, col_count, 2, width)
        rowsum = []
        for a in range(3):
            placed = jnp.pad(kv_parts[a, 0], ((0, 0), (0, 2 * tile_side), (0, 0), (0, 0)))
            placed = placed + jnp.pad(kv_parts[a, 1], ((0, 0), (tile_side, tile_side), (0, 0), (0, 0)))
            placed = placed + jnp.pad(kv_parts[a, 2], ((0, 0), (2 * tile_side, 0), (0, 0), (0, 0)))
            rowsum.append(placed)
        contrib = jnp.concatenate(rowsum, 0).astype(totals.dtype)
        previous = lax.dynamic_slice(totals, cell_at((row_at, 0, 0, group_at)), contrib.shape)
        totals = lax.dynamic_update_slice(totals, previous + contrib, cell_at((row_at, 0, 0, group_at)))
        query_low = query_part.reshape(tile_side, col_count, width).astype(jnp.bfloat16)
        query_grads = lax.dynamic_update_slice(query_grads, query_low, cell_at((row_at, 0, group_at)))
        return ((query_grads, totals), None)
    start = (jnp.zeros(queries.shape, jnp.bfloat16), jnp.zeros((row_count + 2 * tile_side, col_count + 2 * tile_side, 2, features), jnp.float32))
    (query_grads, totals), _ = lax.scan(tile_step, start, jnp.arange(tile_rows * group_count, dtype=jnp.int32))
    return (query_grads, totals)

def reference(queries, key_rows, value_rows, out_grad, pattern, tissue):
    tile_side = TILE_SIDE
    query_list = []
    key_list = []
    value_list = []
    for head in range(HEADS):
        lower = head * HDIM
        upper = lower + HDIM
        stacked = jnp.stack([key_rows[:, :, lower:upper], value_rows[:, :, lower:upper]], 2)
        padded = jnp.pad(stacked, ((tile_side, tile_side), (tile_side, tile_side), (0, 0), (0, 0)))
        query_grads, totals = tile_backward(queries[:, :, lower:upper], padded, out_grad[:, :, lower:upper], pattern, tissue, 0, 0, HDIM)
        inner = totals[tile_side:-tile_side, tile_side:-tile_side].astype(jnp.bfloat16)
        query_list.append(query_grads)
        key_list.append(inner[:, :, 0])
        value_list.append(inner[:, :, 1])
    return (jnp.concatenate(query_list, -1), jnp.concatenate(key_list, -1), jnp.concatenate(value_list, -1))
```

```python
import functools
import math

import jax
import jax.numpy as jnp
from jax import lax
from jax.experimental import pallas as pl
from jax.experimental.pallas import tpu as pltpu
from jax.sharding import PartitionSpec as P

HDIM = 80
TILE_SIDE = 8
LANES = 128
WINDOW = 256
MASKED = -1e30


def plan(half):
    cuts, steps = [0], []
    done_heads, done_lanes = 0, 0
    while cuts[-1] < half:
        stop = min(cuts[-1] + WINDOW, half)
        heads = stop // HDIM
        lanes = half if stop == half else heads * HDIM // LANES * LANES
        steps.append(((cuts[-1], stop - cuts[-1]), (done_heads, heads), (done_lanes, lanes - done_lanes)))
        cuts.append(stop)
        done_heads, done_lanes = heads, lanes
    return steps


def kernel(
    block_count_heads,
    block_count,
    q_ref, k_ref, v_ref, g_ref, pattern_ref, tissue_ref,
    dq_out, dk_out, dv_out,
    qx, gx, kx, vx, bias, key_acc, value_acc, stage, landed, dq_low, dk_low, dv_low,
    in_send, in_recv, own_sem, part_send, part_recv, out_send, out_recv, out_own,
):
    side = TILE_SIDE
    rows, cols, features = q_ref.shape
    half = features // 2
    wide = 2 * cols
    tile_rows, tile_cols = rows // side, wide // side
    near = (tile_rows + 1) * side
    me = lax.axis_index("cols")
    sib = 1 - me
    block = lax.axis_index("rows") * block_count_heads + lax.axis_index("heads")
    has_up, has_down = block > 0, block < block_count - 1

    def at_block(index, core):
        return {"rows": index // block_count_heads, "heads": index % block_count_heads, "cols": core}

    sibling = at_block(block, sib)
    beside = ((block - 1, has_up), (block + 1, has_down))
    mine = pl.ds(pl.multiple_of(me * cols, cols), cols)
    theirs = pl.ds(pl.multiple_of(sib * cols, cols), cols)

    def lanes_of(core, low, width):
        return pl.ds(pl.multiple_of(core * half + low, LANES), width)

    own = [
        pltpu.make_async_copy(src.at[:, :, lanes_of(me, 0, half)], dst, own_sem.at[i])
        for i, (src, dst) in enumerate(
            (
                (q_ref, qx.at[:, mine]),
                (k_ref, kx.at[pl.ds(side, rows), mine]),
                (v_ref, vx.at[pl.ds(side, rows), mine]),
                (g_ref, gx.at[:, mine]),
            )
        )
    ]
    for copy in own:
        copy.start()

    barrier = pltpu.get_barrier_semaphore()
    pl.semaphore_signal(barrier, inc=1, device_id=sibling, device_id_type=pl.DeviceIdType.MESH)
    for index, exists in beside:
        @pl.when(exists)
        def _():
            for core in range(2):
                pl.semaphore_signal(
                    barrier, inc=1, device_id=at_block(index, core), device_id_type=pl.DeviceIdType.MESH
                )
    pl.semaphore_wait(barrier, 1 + 2 * has_up.astype(jnp.int32) + 2 * has_down.astype(jnp.int32))

    def remote(src, dst, send, recv, device):
        return pltpu.make_async_remote_copy(
            src_ref=src, dst_ref=dst, send_sem=send, recv_sem=recv,
            device_id=device, device_id_type=pl.DeviceIdType.MESH,
        )

    steps = plan(half)
    source_rows = (pl.ds(0, side), pl.ds(rows - side, side))
    target_rows = (pl.ds(side + rows, side), pl.ds(0, side))

    def sibling_copies(step, columns):
        low, width = steps[step][0]
        pieces = (
            (q_ref, qx.at[:, columns, pl.ds(low, width)]),
            (k_ref, kx.at[pl.ds(side, rows), columns, pl.ds(low, width)]),
            (v_ref, vx.at[pl.ds(side, rows), columns, pl.ds(low, width)]),
            (g_ref, gx.at[:, columns, pl.ds(low, width)]),
        )
        return [
            remote(src.at[:, :, lanes_of(sib, low, width)], dst,
                   in_send.at[step, i], in_recv.at[step, i], sibling)
            for i, (src, dst) in enumerate(pieces)
        ]

    def halo_copy(step, way, which, target, from_core):
        low, width = steps[step][0]
        src, dst = ((k_ref, kx), (v_ref, vx))[which]
        first = 4 + way * 4 + which * 2
        columns = pl.ds(pl.multiple_of(from_core * cols, cols), cols)
        return remote(
            src.at[source_rows[way], :, lanes_of(target, low, width)],
            dst.at[target_rows[way], columns, pl.ds(low, width)],
            in_send.at[step, first + target], in_recv.at[step, first + from_core],
            at_block(beside[way][0], target),
        )

    for step in range(len(steps)):
        for way in range(2):
            @pl.when(beside[way][1])
            def _():
                for which in range(2):
                    for target in range(2):
                        halo_copy(step, way, which, target, me).start()
        for copy in sibling_copies(step, mine):
            copy.start()

    grid_rows = pattern_ref.shape[0]
    key_col = lax.broadcasted_iota(jnp.int32, (wide, side * wide), 0) // side
    query_col = lax.broadcasted_iota(jnp.int32, (wide, side * wide), 1) % wide // side
    for t in range(tile_rows):
        tile_row = block * tile_rows + t
        for a in range(3):
            key_row = tile_row + a - 1
            inside = ((key_row >= 0) & (key_row < grid_rows)).astype(jnp.int32)
            key_row = jnp.clip(key_row, 0, grid_rows - 1)
            entry = jnp.full((wide, side * wide), MASKED, jnp.float32)
            for at in range(tile_cols):
                bits = pattern_ref[tile_row, at]
                for b in range(3):
                    to = at + b - 1
                    if not 0 <= to < tile_cols:
                        continue
                    if a == 1 and b == 1:
                        value = jnp.float32(0.0)
                    else:
                        ok = ((bits >> (3 * a + b)) & 1) * tissue_ref[key_row, to] * inside
                        value = (1 - ok).astype(jnp.float32) * MASKED
                    entry = jnp.where((key_col == to) & (query_col == at), value, entry)
            bias[t, a] = entry

    key_acc[...] = jnp.zeros_like(key_acc)
    value_acc[...] = jnp.zeros_like(value_acc)
    dq_low[...] = jnp.zeros_like(dq_low)
    for way in range(2):
        @pl.when(jnp.logical_not(beside[1 - way][1]))
        def _():
            kx[target_rows[way]] = jnp.zeros((side, wide, half), kx.dtype)
            vx[target_rows[way]] = jnp.zeros((side, wide, half), vx.dtype)

    scale = 1.0 / math.sqrt(HDIM)
    to_power = scale * math.log2(math.e)
    queries_in, keys_in = side * wide, 3 * side * wide

    def dot(left, right, left_dim, right_dim):
        return lax.dot_general(
            left, right, (((left_dim,), (right_dim,)), ((), ())), preferred_element_type=jnp.float32
        )

    def one(t, head):
        tile = jnp.maximum((HDIM * head + HDIM - 1) // LANES - 1, 0)
        window = pl.ds(pl.multiple_of(tile * LANES, LANES), WINDOW)
        start = HDIM * head - tile * LANES
        lane = lax.broadcasted_iota(jnp.int32, (queries_in, WINDOW), 1)
        in_head = (lane >= start) & (lane < start + HDIM)
        q_rows, k_rows = pl.ds(t * side, side), pl.ds(t * side, 3 * side)
        raw_q = qx[q_rows, :, window].reshape(queries_in, WINDOW)
        raw_g = gx[q_rows, :, window].reshape(queries_in, WINDOW)
        query = jnp.where(in_head, raw_q, jnp.zeros_like(raw_q))
        grad = jnp.where(in_head, raw_g, jnp.zeros_like(raw_g))
        keys = kx[k_rows, :, window].reshape(keys_in, WINDOW)
        values = vx[k_rows, :, window].reshape(keys_in, WINDOW)
        scores = dot(keys, query, 1, 1).reshape(3, side, wide, queries_in) * to_power
        scores = (scores + bias[t][:, None]).reshape(keys_in, queries_in)
        weight_grad = dot(values, grad, 1, 1)
        powers = jnp.exp2(scores - jnp.max(scores, axis=0, keepdims=True))
        weights = powers * (1.0 / jnp.sum(powers, axis=0, keepdims=True))
        row_dot = jnp.sum(weights * weight_grad, axis=0, keepdims=True)
        score_grad = (weights * (weight_grad - row_dot)).astype(jnp.bfloat16)
        weights_low = weights.astype(jnp.bfloat16)
        key_part = dot(score_grad, query, 1, 0).reshape(3 * side, wide, WINDOW)
        value_part = dot(weights_low, grad, 1, 0).reshape(3 * side, wide, WINDOW)
        query_part = (dot(score_grad, keys, 0, 0) * scale).astype(jnp.bfloat16)
        key_acc[k_rows, :, window] += key_part
        value_acc[k_rows, :, window] += value_part
        old = dq_low[q_rows, :, window].reshape(queries_in, WINDOW)
        dq_low[q_rows, :, window] = jnp.where(in_head, query_part, old).reshape(side, wide, WINDOW)

    def part_copy(step, way, which):
        low, width = steps[step][2]
        place = (which, way, slice(None), slice(None), pl.ds(low, width))
        return remote(
            stage.at[place], landed.at[place],
            part_send.at[step, 2 * way + which], part_recv.at[step, 2 * way + which],
            at_block(beside[way][0], me),
        )

    outs = ((dq_low, dq_out), (dk_low, dk_out), (dv_low, dv_out))

    def out_copies(step, i):
        low, width = steps[step][2]
        src, dst = outs[i]
        kept = pltpu.make_async_copy(
            src.at[:, mine, pl.ds(low, width)], dst.at[:, :, lanes_of(me, low, width)], out_own.at[step, i]
        )
        sent = remote(
            src.at[:, theirs, pl.ds(low, width)], dst.at[:, :, lanes_of(me, low, width)],
            out_send.at[step, i], out_recv.at[step, i], sibling,
        )
        return kept, sent

    def out_arrival(step, i):
        low, width = steps[step][2]
        src, dst = outs[i]
        return remote(
            src.at[:, theirs, pl.ds(low, width)], dst.at[:, :, lanes_of(sib, low, width)],
            out_send.at[step, i], out_recv.at[step, i], sibling,
        )

    def finish(step):
        low, width = steps[step][2]
        lanes = pl.ds(low, width)
        for which, (acc, dst, factor) in enumerate(
            ((key_acc, dk_low, scale), (value_acc, dv_low, 1.0))
        ):
            for way in range(2):
                at = pl.ds((rows - side) if way == 0 else 0, side)
                at_acc = pl.ds(rows if way == 0 else side, side)
                total = acc[at_acc, :, lanes] * factor
                exists = beside[1 - way][1]

                @pl.when(exists)
                def _():
                    part_copy(step, way, which).wait_recv()
                    dst[at, :, lanes] = (
                        total + landed[which, way, :, :, lanes].astype(jnp.float32)
                    ).astype(dst.dtype)

                @pl.when(jnp.logical_not(exists))
                def _():
                    dst[at, :, lanes] = total.astype(dst.dtype)
            for copy in out_copies(step, 1 + which):
                copy.start()

    for step, (_, (first, stop), (low, width)) in enumerate(steps):
        if step == 0:
            for copy in own:
                copy.wait()
        for copy in sibling_copies(step, theirs):
            copy.wait_recv()
        for way in range(2):
            @pl.when(beside[1 - way][1])
            def _():
                for which in range(2):
                    for core in range(2):
                        halo_copy(step, way, which, core, core).wait_recv()

        def heads_step(head, carry):
            for t in range(tile_rows):
                one(t, head)
            return carry

        lax.fori_loop(first, stop, heads_step, 0)
        lanes = pl.ds(low, width)
        for way in range(2):
            edge = pl.ds(0 if way == 0 else side + rows, side)

            @pl.when(beside[way][1])
            def _():
                stage[0, way, :, :, lanes] = (key_acc[edge, :, lanes] * scale).astype(stage.dtype)
                part_copy(step, way, 0).start()
                stage[1, way, :, :, lanes] = value_acc[edge, :, lanes].astype(stage.dtype)
                part_copy(step, way, 1).start()
        for copy in out_copies(step, 0):
            copy.start()
        if step > 0:
            finish(step - 1)
    finish(len(steps) - 1)

    for step in range(len(steps)):
        for copy in sibling_copies(step, mine):
            copy.wait_send()
        for way in range(2):
            @pl.when(beside[way][1])
            def _():
                for which in range(2):
                    for target in range(2):
                        halo_copy(step, way, which, target, me).wait_send()
                    part_copy(step, way, which).wait_send()
        for i in range(3):
            kept, sent = out_copies(step, i)
            kept.wait()
            sent.wait_send()
            out_arrival(step, i).wait_recv()


def shards(block_count_heads, block_count, queries, key_rows, value_rows, out_grad, pattern, tissue):
    rows, cols, features = queries.shape
    half, wide, side = features // 2, 2 * cols, TILE_SIDE
    count = len(plan(half))
    low = jnp.bfloat16
    dma = pltpu.SemaphoreType.DMA
    full = jax.ShapeDtypeStruct((rows, cols, features), low)
    return pl.pallas_call(
        functools.partial(kernel, block_count_heads, block_count),
        out_shape=(full, full, full),
        in_specs=[pl.BlockSpec(memory_space=pl.ANY)] * 4 + [pl.BlockSpec(memory_space=pltpu.SMEM)] * 2,
        out_specs=[pl.BlockSpec(memory_space=pl.ANY)] * 3,
        scratch_shapes=[
            pltpu.VMEM((rows, wide, half), low),
            pltpu.VMEM((rows, wide, half), low),
            pltpu.VMEM((rows + 2 * side, wide, half), low),
            pltpu.VMEM((rows + 2 * side, wide, half), low),
            pltpu.VMEM((rows // side, 3, wide, side * wide), jnp.float32),
            pltpu.VMEM((rows + 2 * side, wide, half), jnp.float32),
            pltpu.VMEM((rows + 2 * side, wide, half), jnp.float32),
            pltpu.VMEM((2, 2, side, wide, half), low),
            pltpu.VMEM((2, 2, side, wide, half), low),
            pltpu.VMEM((rows, wide, half), low),
            pltpu.VMEM((rows, wide, half), low),
            pltpu.VMEM((rows, wide, half), low),
            dma((count, 12)),
            dma((count, 12)),
            dma((4,)),
            dma((count, 4)),
            dma((count, 4)),
            dma((count, 3)),
            dma((count, 3)),
            dma((count, 3)),
        ],
        compiler_params=pltpu.CompilerParams(
            collective_id=0, has_side_effects=True, vmem_limit_bytes=48 * 1024 * 1024
        ),
    )(queries, key_rows, value_rows, out_grad, pattern, tissue)


def solution(mesh):
    split = P(("rows", "heads"), "cols", None)
    heads = mesh.shape["heads"]
    return jax.shard_map(
        functools.partial(shards, heads, heads * mesh.shape["rows"]),
        mesh=mesh,
        in_specs=(split, split, split, split, P(), P()),
        out_specs=(split, split, split),
        check_vma=False,
    )
```

```python
import functools
import math

import jax
import jax.numpy as jnp
from jax import lax
from jax.experimental import pallas as pl
from jax.experimental.pallas import tpu as pltpu
from jax.sharding import PartitionSpec as P

HDIM = 80
TILE_SIDE = 8
LANES = 128
WINDOW = 256
MASKED = -1e30


def plan(half):
    cuts, steps = [0], []
    done_heads, done_lanes = 0, 0
    while cuts[-1] < half:
        stop = min(cuts[-1] + WINDOW, half)
        heads = stop // HDIM
        lanes = half if stop == half else heads * HDIM // LANES * LANES
        steps.append(((cuts[-1], stop - cuts[-1]), (done_heads, heads), (done_lanes, lanes - done_lanes)))
        cuts.append(stop)
        done_heads, done_lanes = heads, lanes
    return steps


def kernel(
    block_count_heads,
    block_count,
    q_ref, k_ref, v_ref, g_ref, pattern_ref, tissue_ref,
    dq_out, dk_out, dv_out,
    qx, gx, kx, vx, bias, query_acc, key_acc, value_acc, stats, stats_in, stage, landed,
    dq_low, dk_low, dv_low,
    in_send, in_recv, own_sem, stat_send, stat_recv, part_send, part_recv, out_send, out_recv, out_own,
):
    side = TILE_SIDE
    rows, cols, features = q_ref.shape
    half = features // 2
    wide = 2 * cols
    tile_rows, tile_cols = rows // side, wide // side
    me = lax.axis_index("cols")
    sib = 1 - me
    block = lax.axis_index("rows") * block_count_heads + lax.axis_index("heads")
    has_up, has_down = block > 0, block < block_count - 1

    def at_block(index, core):
        return {"rows": index // block_count_heads, "heads": index % block_count_heads, "cols": core}

    sibling = at_block(block, sib)
    beside = ((block - 1, has_up), (block + 1, has_down))
    mine = pl.ds(pl.multiple_of(me * cols, cols), cols)
    theirs = pl.ds(pl.multiple_of(sib * cols, cols), cols)

    def lanes_of(core, low, width):
        return pl.ds(pl.multiple_of(core * half + low, LANES), width)

    own = [
        pltpu.make_async_copy(src.at[:, :, lanes_of(me, 0, half)], dst, own_sem.at[i])
        for i, (src, dst) in enumerate(
            (
                (q_ref, qx.at[pl.ds(side, rows), mine]),
                (k_ref, kx.at[:, mine]),
                (v_ref, vx.at[:, mine]),
                (g_ref, gx.at[pl.ds(side, rows), mine]),
            )
        )
    ]
    for copy in own:
        copy.start()

    barrier = pltpu.get_barrier_semaphore()
    pl.semaphore_signal(barrier, inc=1, device_id=sibling, device_id_type=pl.DeviceIdType.MESH)
    for index, exists in beside:
        @pl.when(exists)
        def _():
            for core in range(2):
                pl.semaphore_signal(
                    barrier, inc=1, device_id=at_block(index, core), device_id_type=pl.DeviceIdType.MESH
                )
    pl.semaphore_wait(barrier, 1 + 2 * has_up.astype(jnp.int32) + 2 * has_down.astype(jnp.int32))

    def remote(src, dst, send, recv, device):
        return pltpu.make_async_remote_copy(
            src_ref=src, dst_ref=dst, send_sem=send, recv_sem=recv,
            device_id=device, device_id_type=pl.DeviceIdType.MESH,
        )

    steps = plan(half)
    source_rows = (pl.ds(0, side), pl.ds(rows - side, side))
    target_rows = (pl.ds(side + rows, side), pl.ds(0, side))

    def sibling_copies(step, columns):
        low, width = steps[step][0]
        pieces = (
            (q_ref, qx.at[pl.ds(side, rows), columns, pl.ds(low, width)]),
            (k_ref, kx.at[:, columns, pl.ds(low, width)]),
            (v_ref, vx.at[:, columns, pl.ds(low, width)]),
            (g_ref, gx.at[pl.ds(side, rows), columns, pl.ds(low, width)]),
        )
        return [
            remote(src.at[:, :, lanes_of(sib, low, width)], dst,
                   in_send.at[step, i], in_recv.at[step, i], sibling)
            for i, (src, dst) in enumerate(pieces)
        ]

    def halo_copy(step, way, which, target, from_core):
        low, width = steps[step][0]
        src, dst = ((q_ref, qx), (g_ref, gx))[which]
        first = 4 + way * 4 + which * 2
        columns = pl.ds(pl.multiple_of(from_core * cols, cols), cols)
        return remote(
            src.at[source_rows[way], :, lanes_of(target, low, width)],
            dst.at[target_rows[way], columns, pl.ds(low, width)],
            in_send.at[step, first + target], in_recv.at[step, first + from_core],
            at_block(beside[way][0], target),
        )

    for step in range(len(steps)):
        for way in range(2):
            @pl.when(beside[way][1])
            def _():
                for which in range(2):
                    for target in range(2):
                        halo_copy(step, way, which, target, me).start()
        for copy in sibling_copies(step, mine):
            copy.start()

    query_rows = tile_rows + 2
    reach = [[at for at in (u - 2, u - 1, u) if 0 <= at < tile_rows] for u in range(query_rows)]
    first_mask = [sum(len(r) for r in reach[:u]) for u in range(query_rows)]
    grid_rows = pattern_ref.shape[0]
    key_col = lax.broadcasted_iota(jnp.int32, (wide, side * wide), 0) // side
    query_col = lax.broadcasted_iota(jnp.int32, (wide, side * wide), 1) % wide // side
    for u in range(query_rows):
        query_row = block * tile_rows + u - 1
        inside = ((query_row >= 0) & (query_row < grid_rows)).astype(jnp.int32)
        query_row = jnp.clip(query_row, 0, grid_rows - 1)
        for i, key_at in enumerate(reach[u]):
            a = key_at - u + 2
            key_row = block * tile_rows + key_at
            entry = jnp.full((wide, side * wide), MASKED, jnp.float32)
            for at in range(tile_cols):
                bits = pattern_ref[query_row, at]
                for b in range(3):
                    to = at + b - 1
                    if not 0 <= to < tile_cols:
                        continue
                    if a == 1 and b == 1:
                        value = jnp.float32(0.0)
                    else:
                        ok = ((bits >> (3 * a + b)) & 1) * tissue_ref[key_row, to] * inside
                        value = (1 - ok).astype(jnp.float32) * MASKED
                    entry = jnp.where((key_col == to) & (query_col == at), value, entry)
            bias[first_mask[u] + i] = entry

    key_acc[...] = jnp.zeros_like(key_acc)
    value_acc[...] = jnp.zeros_like(value_acc)
    query_acc[...] = jnp.zeros_like(query_acc)
    stats[...] = jnp.zeros_like(stats)
    for way in range(2):
        @pl.when(jnp.logical_not(beside[1 - way][1]))
        def _():
            qx[target_rows[way]] = jnp.zeros((side, wide, half), qx.dtype)
            gx[target_rows[way]] = jnp.zeros((side, wide, half), gx.dtype)
            for step in range(len(steps)):
                for i in range(2):
                    stats_in[2 - 2 * way + i, step] = jnp.full(stats_in.shape[2:], MASKED, jnp.float32)

    scale = 1.0 / math.sqrt(HDIM)
    to_power = scale * math.log2(math.e)
    queries_in = side * wide

    def dot(left, right, left_dim, right_dim):
        return lax.dot_general(
            left, right, (((left_dim,), (right_dim,)), ((), ())), preferred_element_type=jnp.float32
        )

    def prepare(head):
        tile = jnp.maximum((HDIM * head + HDIM - 1) // LANES - 1, 0)
        window = pl.ds(pl.multiple_of(tile * LANES, LANES), WINDOW)
        start = HDIM * head - tile * LANES
        lane = lax.broadcasted_iota(jnp.int32, (queries_in, WINDOW), 1)
        return window, (lane >= start) & (lane < start + HDIM)

    def pair(u, window, in_head):
        count = len(reach[u])
        keys_in = count * queries_in
        q_rows, k_rows = pl.ds(u * side, side), pl.ds(reach[u][0] * side, count * side)
        raw_q = qx[q_rows, :, window].reshape(queries_in, WINDOW)
        raw_g = gx[q_rows, :, window].reshape(queries_in, WINDOW)
        query = jnp.where(in_head, raw_q, jnp.zeros_like(raw_q))
        grad = jnp.where(in_head, raw_g, jnp.zeros_like(raw_g))
        keys = kx[k_rows, :, window].reshape(keys_in, WINDOW)
        values = vx[k_rows, :, window].reshape(keys_in, WINDOW)
        scores = dot(keys, query, 1, 1).reshape(count, side, wide, queries_in) * to_power
        masks = bias[first_mask[u] : first_mask[u] + count]
        scores = (scores + masks[:, None]).reshape(keys_in, queries_in)
        return q_rows, k_rows, query, grad, keys, scores, dot(values, grad, 1, 1)

    def measure(u, step, at, window, in_head):
        _, _, _, _, _, scores, weight_grad = pair(u, window, in_head)
        top = jnp.max(scores, axis=0, keepdims=True)
        powers = jnp.exp2(scores - top)
        total = jnp.sum(powers, axis=0, keepdims=True)
        part = jnp.sum(powers * weight_grad, axis=0, keepdims=True)
        stats[u, step, pl.ds(2 * at, 1), :] = top + jnp.log2(total)
        stats[u, step, pl.ds(2 * at + 1, 1), :] = part / total

    def gradients(u, step, at, window, in_head):
        q_rows, k_rows, query, grad, keys, scores, weight_grad = pair(u, window, in_head)
        here, there = stats[u, step, pl.ds(2 * at, 1), :], stats_in[u, step, pl.ds(2 * at, 1), :]
        top = jnp.maximum(here, there)
        power_here, power_there = jnp.exp2(here - top), jnp.exp2(there - top)
        total = power_here + power_there
        row_dot = (
            power_here * stats[u, step, pl.ds(2 * at + 1, 1), :]
            + power_there * stats_in[u, step, pl.ds(2 * at + 1, 1), :]
        ) / total
        weights = jnp.exp2(scores - top) * (1.0 / total)
        score_grad = (weights * (weight_grad - row_dot)).astype(jnp.bfloat16)
        weights_low = weights.astype(jnp.bfloat16)
        shape = (len(reach[u]) * side, wide, WINDOW)
        key_acc[k_rows, :, window] += dot(score_grad, query, 1, 0).reshape(shape)
        value_acc[k_rows, :, window] += dot(weights_low, grad, 1, 0).reshape(shape)
        query_part = dot(score_grad, keys, 0, 0) * scale
        old = query_acc[q_rows, :, window].reshape(queries_in, WINDOW)
        query_acc[q_rows, :, window] = jnp.where(in_head, query_part, old).reshape(side, wide, WINDOW)

    def each_head(step, act):
        first, stop = steps[step][1]

        def body(head, carry):
            window, in_head = prepare(head)
            for u in range(query_rows):
                act(u, step, head - first, window, in_head)
            return carry

        lax.fori_loop(first, stop, body, 0)

    def stat_copy(step, way):
        here, there = (0, query_rows - 2) if way == 0 else (query_rows - 2, 0)
        return remote(
            stats.at[pl.ds(here, 2), step], stats_in.at[pl.ds(there, 2), step],
            stat_send.at[step, way], stat_recv.at[step, way], at_block(beside[way][0], me),
        )

    def part_copy(step, way):
        low, width = steps[step][2]
        place = (way, slice(None), slice(None), pl.ds(low, width))
        return remote(
            stage.at[place], landed.at[place], part_send.at[step, way], part_recv.at[step, way],
            at_block(beside[way][0], me),
        )

    outs = ((dq_low, dq_out), (dk_low, dk_out), (dv_low, dv_out))

    def out_copies(step, i):
        low, width = steps[step][2]
        src, dst = outs[i]
        kept = pltpu.make_async_copy(
            src.at[:, mine, pl.ds(low, width)], dst.at[:, :, lanes_of(me, low, width)], out_own.at[step, i]
        )
        sent = remote(
            src.at[:, theirs, pl.ds(low, width)], dst.at[:, :, lanes_of(me, low, width)],
            out_send.at[step, i], out_recv.at[step, i], sibling,
        )
        return kept, sent

    def out_arrival(step, i):
        low, width = steps[step][2]
        src, dst = outs[i]
        return remote(
            src.at[:, theirs, pl.ds(low, width)], dst.at[:, :, lanes_of(sib, low, width)],
            out_send.at[step, i], out_recv.at[step, i], sibling,
        )

    def work(step):
        for way in range(2):
            @pl.when(beside[1 - way][1])
            def _():
                stat_copy(step, way).wait_recv()
        each_head(step, gradients)
        low, width = steps[step][2]
        lanes = pl.ds(low, width)
        for way in range(2):
            edge = pl.ds(0 if way == 0 else side + rows, side)

            @pl.when(beside[way][1])
            def _():
                stage[way, :, :, lanes] = query_acc[edge, :, lanes].astype(stage.dtype)
                part_copy(step, way).start()
        dk_low[:, :, lanes] = (key_acc[:, :, lanes] * scale).astype(dk_low.dtype)
        dv_low[:, :, lanes] = value_acc[:, :, lanes].astype(dv_low.dtype)
        for i in (1, 2):
            for copy in out_copies(step, i):
                copy.start()

    def finish(step):
        low, width = steps[step][2]
        lanes = pl.ds(low, width)
        for way in range(2):
            at = pl.ds((rows - side) if way == 0 else 0, side)
            total = query_acc[pl.ds(rows if way == 0 else side, side), :, lanes]
            exists = beside[1 - way][1]

            @pl.when(exists)
            def _():
                part_copy(step, way).wait_recv()
                dq_low[at, :, lanes] = (total + landed[way, :, :, lanes].astype(jnp.float32)).astype(dq_low.dtype)

            @pl.when(jnp.logical_not(exists))
            def _():
                dq_low[at, :, lanes] = total.astype(dq_low.dtype)
        for copy in out_copies(step, 0):
            copy.start()

    for step in range(len(steps)):
        if step == 0:
            for copy in own:
                copy.wait()
        for copy in sibling_copies(step, theirs):
            copy.wait_recv()
        for way in range(2):
            @pl.when(beside[1 - way][1])
            def _():
                for which in range(2):
                    for core in range(2):
                        halo_copy(step, way, which, core, core).wait_recv()
        each_head(step, measure)
        for way in range(2):
            @pl.when(beside[way][1])
            def _():
                stat_copy(step, way).start()
        if step > 0:
            work(step - 1)
        if step > 1:
            finish(step - 2)
    work(len(steps) - 1)
    for step in range(max(len(steps) - 2, 0), len(steps)):
        finish(step)

    for step in range(len(steps)):
        for copy in sibling_copies(step, mine):
            copy.wait_send()
        for way in range(2):
            @pl.when(beside[way][1])
            def _():
                for which in range(2):
                    for target in range(2):
                        halo_copy(step, way, which, target, me).wait_send()
                stat_copy(step, way).wait_send()
                part_copy(step, way).wait_send()
        for i in range(3):
            kept, sent = out_copies(step, i)
            kept.wait()
            sent.wait_send()
            out_arrival(step, i).wait_recv()


def shards(block_count_heads, block_count, queries, key_rows, value_rows, out_grad, pattern, tissue):
    rows, cols, features = queries.shape
    half, wide, side = features // 2, 2 * cols, TILE_SIDE
    count = len(plan(half))
    low = jnp.bfloat16
    dma = pltpu.SemaphoreType.DMA
    full = jax.ShapeDtypeStruct((rows, cols, features), low)
    return pl.pallas_call(
        functools.partial(kernel, block_count_heads, block_count),
        out_shape=(full, full, full),
        in_specs=[pl.BlockSpec(memory_space=pl.ANY)] * 4 + [pl.BlockSpec(memory_space=pltpu.SMEM)] * 2,
        out_specs=[pl.BlockSpec(memory_space=pl.ANY)] * 3,
        scratch_shapes=[
            pltpu.VMEM((rows + 2 * side, wide, half), low),
            pltpu.VMEM((rows + 2 * side, wide, half), low),
            pltpu.VMEM((rows, wide, half), low),
            pltpu.VMEM((rows, wide, half), low),
            pltpu.VMEM((3 * (rows // side), wide, side * wide), jnp.float32),
            pltpu.VMEM((rows + 2 * side, wide, half), jnp.float32),
            pltpu.VMEM((rows, wide, half), jnp.float32),
            pltpu.VMEM((rows, wide, half), jnp.float32),
            pltpu.VMEM((rows // side + 2, count, 8, side * wide), jnp.float32),
            pltpu.VMEM((rows // side + 2, count, 8, side * wide), jnp.float32),
            pltpu.VMEM((2, side, wide, half), low),
            pltpu.VMEM((2, side, wide, half), low),
            pltpu.VMEM((rows, wide, half), low),
            pltpu.VMEM((rows, wide, half), low),
            pltpu.VMEM((rows, wide, half), low),
            dma((count, 12)),
            dma((count, 12)),
            dma((4,)),
            dma((count, 2)),
            dma((count, 2)),
            dma((count, 2)),
            dma((count, 2)),
            dma((count, 3)),
            dma((count, 3)),
            dma((count, 3)),
        ],
        compiler_params=pltpu.CompilerParams(
            collective_id=0, has_side_effects=True, vmem_limit_bytes=60 * 1024 * 1024
        ),
    )(queries, key_rows, value_rows, out_grad, pattern, tissue)


def solution(mesh):
    split = P(("rows", "heads"), "cols", None)
    heads = mesh.shape["heads"]
    return jax.shard_map(
        functools.partial(shards, heads, heads * mesh.shape["rows"]),
        mesh=mesh,
        in_specs=(split, split, split, split, P(), P()),
        out_specs=(split, split, split),
        check_vma=False,
    )
```

```python
import functools
import math

import jax
import jax.numpy as jnp
from jax import lax
from jax.experimental import pallas as pl
from jax.experimental.pallas import tpu as pltpu
from jax.sharding import PartitionSpec as P

HDIM = 80
TILE_SIDE = 8
LANES = 128
WINDOW = 256
MASKED = -1e30


def plan(half):
    steps, arrived, done_heads, done_lanes = [], 0, 0, 0
    while done_lanes < half:
        stop = min(arrived + WINDOW, half)
        heads = stop // HDIM
        lanes = heads * HDIM // LANES * LANES
        steps.append(((arrived, stop - arrived), (done_heads, heads), (done_lanes, lanes - done_lanes)))
        arrived, done_heads, done_lanes = stop, heads, lanes
    return steps


def kernel(
    block_count_heads,
    block_count,
    q_ref, k_ref, v_ref, g_ref, pattern_in, tissue_in,
    dq_out, dk_out, dv_out,
    qx, gx, kx, vx, bias, query_acc, key_acc, value_acc, stats, stats_in, stage, landed,
    dq_low, dk_low, dv_low, pattern_ref, tissue_ref,
    in_send, in_recv, own_sem, stat_send, stat_recv, part_send, part_recv, out_send, out_recv, out_own,
):
    side = TILE_SIDE
    rows, cols, features = q_ref.shape
    half = features // 2
    wide = 2 * cols
    tile_rows, tile_cols = rows // side, wide // side
    me = lax.axis_index("cols")
    sib = 1 - me
    block = lax.axis_index("rows") * block_count_heads + lax.axis_index("heads")
    has_up, has_down = block > 0, block < block_count - 1

    def at_block(index, core):
        return {"rows": index // block_count_heads, "heads": index % block_count_heads, "cols": core}

    sibling = at_block(block, sib)
    beside = ((block - 1, has_up), (block + 1, has_down))
    mine = pl.ds(pl.multiple_of(me * cols, cols), cols)
    theirs = pl.ds(pl.multiple_of(sib * cols, cols), cols)

    def lanes_of(core, low, width):
        return pl.ds(pl.multiple_of(core * half + low, LANES), width)

    own = [
        pltpu.make_async_copy(src.at[:, :, lanes_of(me, 0, half)], dst, own_sem.at[i])
        for i, (src, dst) in enumerate(
            (
                (q_ref, qx.at[pl.ds(side, rows), mine]),
                (k_ref, kx.at[:, mine]),
                (v_ref, vx.at[:, mine]),
                (g_ref, gx.at[pl.ds(side, rows), mine]),
            )
        )
    ]
    small = [
        pltpu.make_async_copy(src, dst, own_sem.at[4 + i])
        for i, (src, dst) in enumerate(((pattern_in, pattern_ref), (tissue_in, tissue_ref)))
    ]
    for copy in own + small:
        copy.start()

    barrier = pltpu.get_barrier_semaphore()
    pl.semaphore_signal(barrier, inc=1, device_id=sibling, device_id_type=pl.DeviceIdType.MESH)
    for index, exists in beside:
        @pl.when(exists)
        def _():
            for core in range(2):
                pl.semaphore_signal(
                    barrier, inc=1, device_id=at_block(index, core), device_id_type=pl.DeviceIdType.MESH
                )
    pl.semaphore_wait(barrier, 1 + 2 * has_up.astype(jnp.int32) + 2 * has_down.astype(jnp.int32))

    def remote(src, dst, send, recv, device):
        return pltpu.make_async_remote_copy(
            src_ref=src, dst_ref=dst, send_sem=send, recv_sem=recv,
            device_id=device, device_id_type=pl.DeviceIdType.MESH,
        )

    steps = plan(half)
    source_rows = (pl.ds(0, side), pl.ds(rows - side, side))
    target_rows = (pl.ds(side + rows, side), pl.ds(0, side))

    def sibling_copies(step, columns):
        low, width = steps[step][0]
        if not width:
            return []
        pieces = (
            (q_ref, qx.at[pl.ds(side, rows), columns, pl.ds(low, width)]),
            (k_ref, kx.at[:, columns, pl.ds(low, width)]),
            (v_ref, vx.at[:, columns, pl.ds(low, width)]),
            (g_ref, gx.at[pl.ds(side, rows), columns, pl.ds(low, width)]),
        )
        return [
            remote(src.at[:, :, lanes_of(sib, low, width)], dst,
                   in_send.at[step, i], in_recv.at[step, i], sibling)
            for i, (src, dst) in enumerate(pieces)
        ]

    def halo_copy(step, way, which, target, from_core):
        low, width = steps[step][0]
        src, dst = ((q_ref, qx), (g_ref, gx))[which]
        first = 4 + way * 4 + which * 2
        columns = pl.ds(pl.multiple_of(from_core * cols, cols), cols)
        return remote(
            src.at[source_rows[way], :, lanes_of(target, low, width)],
            dst.at[target_rows[way], columns, pl.ds(low, width)],
            in_send.at[step, first + target], in_recv.at[step, first + from_core],
            at_block(beside[way][0], target),
        )

    for step in range(len(steps)):
        for way in range(2):
            @pl.when(beside[way][1])
            def _():
                for which in range(2 if steps[step][0][1] else 0):
                    for target in range(2):
                        halo_copy(step, way, which, target, me).start()
        for copy in sibling_copies(step, mine):
            copy.start()

    query_rows = tile_rows + 2
    reach = [[at for at in (u - 2, u - 1, u) if 0 <= at < tile_rows] for u in range(query_rows)]
    first_mask = [sum(len(r) for r in reach[:u]) for u in range(query_rows)]
    for copy in small:
        copy.wait()
    grid_rows = pattern_ref.shape[0]
    key_col = lax.broadcasted_iota(jnp.int32, (wide, side * wide), 0) // side
    query_col = lax.broadcasted_iota(jnp.int32, (wide, side * wide), 1) % wide // side
    for u in range(query_rows):
        query_row = block * tile_rows + u - 1
        inside = ((query_row >= 0) & (query_row < grid_rows)).astype(jnp.int32)
        query_row = jnp.clip(query_row, 0, grid_rows - 1)
        for i, key_at in enumerate(reach[u]):
            a = key_at - u + 2
            key_row = block * tile_rows + key_at
            entry = jnp.full((wide, side * wide), MASKED, jnp.float32)
            for at in range(tile_cols):
                bits = pattern_ref[query_row, at]
                for b in range(3):
                    to = at + b - 1
                    if not 0 <= to < tile_cols:
                        continue
                    if a == 1 and b == 1:
                        value = jnp.float32(0.0)
                    else:
                        ok = ((bits >> (3 * a + b)) & 1) * tissue_ref[key_row, to] * inside
                        value = (1 - ok).astype(jnp.float32) * MASKED
                    entry = jnp.where((key_col == to) & (query_col == at), value, entry)
            bias[first_mask[u] + i] = entry

    key_acc[...] = jnp.zeros_like(key_acc)
    value_acc[...] = jnp.zeros_like(value_acc)
    query_acc[...] = jnp.zeros_like(query_acc)
    stats[...] = jnp.zeros_like(stats)
    for way in range(2):
        @pl.when(jnp.logical_not(beside[1 - way][1]))
        def _():
            qx[target_rows[way]] = jnp.zeros((side, wide, half), qx.dtype)
            gx[target_rows[way]] = jnp.zeros((side, wide, half), gx.dtype)
            for step in range(len(steps)):
                for i in range(2):
                    stats_in[2 - 2 * way + i, step] = jnp.full(stats_in.shape[2:], MASKED, jnp.float32)

    scale = 1.0 / math.sqrt(HDIM)
    to_power = scale * math.log2(math.e)
    queries_in = side * wide

    def dot(left, right, left_dim, right_dim):
        return lax.dot_general(
            left, right, (((left_dim,), (right_dim,)), ((), ())), preferred_element_type=jnp.float32
        )

    def prepare(head):
        tile = jnp.maximum((HDIM * head + HDIM - 1) // LANES - 1, 0)
        window = pl.ds(pl.multiple_of(tile * LANES, LANES), WINDOW)
        start = HDIM * head - tile * LANES
        lane = lax.broadcasted_iota(jnp.int32, (queries_in, WINDOW), 1)
        return window, (lane >= start) & (lane < start + HDIM)

    def pair(u, window, in_head):
        count = len(reach[u])
        keys_in = count * queries_in
        q_rows, k_rows = pl.ds(u * side, side), pl.ds(reach[u][0] * side, count * side)
        raw_q = qx[q_rows, :, window].reshape(queries_in, WINDOW)
        raw_g = gx[q_rows, :, window].reshape(queries_in, WINDOW)
        query = jnp.where(in_head, raw_q, jnp.zeros_like(raw_q))
        grad = jnp.where(in_head, raw_g, jnp.zeros_like(raw_g))
        keys = kx[k_rows, :, window].reshape(keys_in, WINDOW)
        values = vx[k_rows, :, window].reshape(keys_in, WINDOW)
        scores = dot(keys, query, 1, 1).reshape(count, side, wide, queries_in) * to_power
        masks = bias[first_mask[u] : first_mask[u] + count]
        scores = (scores + masks[:, None]).reshape(keys_in, queries_in)
        return q_rows, k_rows, query, grad, keys, scores, dot(values, grad, 1, 1)

    def measure(u, step, at, window, in_head):
        _, _, _, _, _, scores, weight_grad = pair(u, window, in_head)
        top = jnp.max(scores, axis=0, keepdims=True)
        powers = jnp.exp2(scores - top)
        total = jnp.sum(powers, axis=0, keepdims=True)
        part = jnp.sum(powers * weight_grad, axis=0, keepdims=True)
        stats[u, step, pl.ds(2 * at, 1), :] = top + jnp.log2(total)
        stats[u, step, pl.ds(2 * at + 1, 1), :] = part / total

    def gradients(u, step, at, window, in_head):
        q_rows, k_rows, query, grad, keys, scores, weight_grad = pair(u, window, in_head)
        here, there = stats[u, step, pl.ds(2 * at, 1), :], stats_in[u, step, pl.ds(2 * at, 1), :]
        top = jnp.maximum(here, there)
        power_here, power_there = jnp.exp2(here - top), jnp.exp2(there - top)
        total = power_here + power_there
        row_dot = (
            power_here * stats[u, step, pl.ds(2 * at + 1, 1), :]
            + power_there * stats_in[u, step, pl.ds(2 * at + 1, 1), :]
        ) / total
        weights = jnp.exp2(scores - top) * (1.0 / total)
        score_grad = (weights * (weight_grad - row_dot)).astype(jnp.bfloat16)
        weights_low = weights.astype(jnp.bfloat16)
        shape = (len(reach[u]) * side, wide, WINDOW)
        key_acc[k_rows, :, window] += dot(score_grad, query, 1, 0).reshape(shape)
        value_acc[k_rows, :, window] += dot(weights_low, grad, 1, 0).reshape(shape)
        query_part = dot(score_grad, keys, 0, 0) * scale
        old = query_acc[q_rows, :, window].reshape(queries_in, WINDOW)
        query_acc[q_rows, :, window] = jnp.where(in_head, query_part, old).reshape(side, wide, WINDOW)

    def each_head(step, act):
        first, stop = steps[step][1]

        def body(head, carry):
            window, in_head = prepare(head)
            for u in range(query_rows):
                act(u, step, head - first, window, in_head)
            return carry

        lax.fori_loop(first, stop, body, 0, unroll=True)

    def stat_copy(step, way):
        here, there = (0, query_rows - 2) if way == 0 else (query_rows - 2, 0)
        return remote(
            stats.at[pl.ds(here, 2), step], stats_in.at[pl.ds(there, 2), step],
            stat_send.at[step, way], stat_recv.at[step, way], at_block(beside[way][0], me),
        )

    def part_copy(step, way):
        low, width = steps[step][2]
        place = (way, slice(None), slice(None), pl.ds(low, width))
        return remote(
            stage.at[place], landed.at[place], part_send.at[step, way], part_recv.at[step, way],
            at_block(beside[way][0], me),
        )

    outs = ((dq_low, dq_out), (dk_low, dk_out), (dv_low, dv_out))

    def out_copies(step, i):
        low, width = steps[step][2]
        src, dst = outs[i]
        kept = pltpu.make_async_copy(
            src.at[:, mine, pl.ds(low, width)], dst.at[:, :, lanes_of(me, low, width)], out_own.at[step, i]
        )
        sent = remote(
            src.at[:, theirs, pl.ds(low, width)], dst.at[:, :, lanes_of(me, low, width)],
            out_send.at[step, i], out_recv.at[step, i], sibling,
        )
        return kept, sent

    def out_arrival(step, i):
        low, width = steps[step][2]
        src, dst = outs[i]
        return remote(
            src.at[:, theirs, pl.ds(low, width)], dst.at[:, :, lanes_of(sib, low, width)],
            out_send.at[step, i], out_recv.at[step, i], sibling,
        )

    def work(step):
        for way in range(2):
            @pl.when(beside[1 - way][1])
            def _():
                stat_copy(step, way).wait_recv()
        each_head(step, gradients)
        low, width = steps[step][2]
        lanes = pl.ds(low, width)
        for way in range(2):
            edge = pl.ds(0 if way == 0 else side + rows, side)

            @pl.when(beside[way][1])
            def _():
                stage[way, :, :, lanes] = query_acc[edge, :, lanes].astype(stage.dtype)
                part_copy(step, way).start()
        dk_low[:, :, lanes] = (key_acc[:, :, lanes] * scale).astype(dk_low.dtype)
        dv_low[:, :, lanes] = value_acc[:, :, lanes].astype(dv_low.dtype)
        for i in (1, 2):
            for copy in out_copies(step, i):
                copy.start()

    def finish(step):
        low, width = steps[step][2]
        lanes = pl.ds(low, width)
        for way in range(2):
            at = pl.ds((rows - side) if way == 0 else 0, side)
            total = query_acc[pl.ds(rows if way == 0 else side, side), :, lanes]
            exists = beside[1 - way][1]

            @pl.when(exists)
            def _():
                part_copy(step, way).wait_recv()
                dq_low[at, :, lanes] = (total + landed[way, :, :, lanes].astype(jnp.float32)).astype(dq_low.dtype)

            @pl.when(jnp.logical_not(exists))
            def _():
                dq_low[at, :, lanes] = total.astype(dq_low.dtype)
        for copy in out_copies(step, 0):
            copy.start()

    for step in range(len(steps)):
        if step == 0:
            for copy in own:
                copy.wait()
        for copy in sibling_copies(step, theirs):
            copy.wait_recv()
        for way in range(2):
            @pl.when(beside[1 - way][1])
            def _():
                for which in range(2 if steps[step][0][1] else 0):
                    for core in range(2):
                        halo_copy(step, way, which, core, core).wait_recv()
        each_head(step, measure)
        for way in range(2):
            @pl.when(beside[way][1])
            def _():
                stat_copy(step, way).start()
        if step > 0:
            work(step - 1)
        if step > 1:
            finish(step - 2)
    work(len(steps) - 1)
    for step in range(max(len(steps) - 2, 0), len(steps)):
        finish(step)

    for step in range(len(steps)):
        for copy in sibling_copies(step, mine):
            copy.wait_send()
        for way in range(2):
            @pl.when(beside[way][1])
            def _():
                for which in range(2 if steps[step][0][1] else 0):
                    for target in range(2):
                        halo_copy(step, way, which, target, me).wait_send()
                stat_copy(step, way).wait_send()
                part_copy(step, way).wait_send()
        for i in range(3):
            kept, sent = out_copies(step, i)
            kept.wait()
            sent.wait_send()
            out_arrival(step, i).wait_recv()


def shards(block_count_heads, block_count, queries, key_rows, value_rows, out_grad, pattern, tissue):
    rows, cols, features = queries.shape
    half, wide, side = features // 2, 2 * cols, TILE_SIDE
    count = len(plan(half))
    low = jnp.bfloat16
    dma = pltpu.SemaphoreType.DMA
    full = jax.ShapeDtypeStruct((rows, cols, features), low)
    return pl.pallas_call(
        functools.partial(kernel, block_count_heads, block_count),
        out_shape=(full, full, full),
        in_specs=[pl.BlockSpec(memory_space=pl.ANY)] * 6,
        out_specs=[pl.BlockSpec(memory_space=pl.ANY)] * 3,
        scratch_shapes=[
            pltpu.VMEM((rows + 2 * side, wide, half), low),
            pltpu.VMEM((rows + 2 * side, wide, half), low),
            pltpu.VMEM((rows, wide, half), low),
            pltpu.VMEM((rows, wide, half), low),
            pltpu.VMEM((3 * (rows // side), wide, side * wide), jnp.float32),
            pltpu.VMEM((rows + 2 * side, wide, half), jnp.float32),
            pltpu.VMEM((rows, wide, half), jnp.float32),
            pltpu.VMEM((rows, wide, half), jnp.float32),
            pltpu.VMEM((rows // side + 2, count, 8, side * wide), jnp.float32),
            pltpu.VMEM((rows // side + 2, count, 8, side * wide), jnp.float32),
            pltpu.VMEM((2, side, wide, half), low),
            pltpu.VMEM((2, side, wide, half), low),
            pltpu.VMEM((rows, wide, half), low),
            pltpu.VMEM((rows, wide, half), low),
            pltpu.VMEM((rows, wide, half), low),
            pltpu.SMEM(pattern.shape, pattern.dtype),
            pltpu.SMEM(tissue.shape, tissue.dtype),
            dma((count, 12)),
            dma((count, 12)),
            dma((6,)),
            dma((count, 2)),
            dma((count, 2)),
            dma((count, 2)),
            dma((count, 2)),
            dma((count, 3)),
            dma((count, 3)),
            dma((count, 3)),
        ],
        compiler_params=pltpu.CompilerParams(
            collective_id=0, has_side_effects=True, vmem_limit_bytes=60 * 1024 * 1024
        ),
    )(queries, key_rows, value_rows, out_grad, pattern, tissue)


def solution(mesh):
    split = P(("rows", "heads"), "cols", None)
    heads = mesh.shape["heads"]
    return jax.shard_map(
        functools.partial(shards, heads, heads * mesh.shape["rows"]),
        mesh=mesh,
        in_specs=(split, split, split, split, P(), P()),
        out_specs=(split, split, split),
        check_vma=False,
    )
```
